256 devices in a mesh: dp: 16 (over x, z_hi), expert: 16 (over y, z_lo, core).
Axes of the slice: x: 4, y: 4, z: 8 (z_hi: 4, z_lo: 2; z = z_hi * 2 + z_lo), core: 2. Of those that a mesh axis runs over, the one named last changes fastest.
Arguments:
- tokens: bfloat16 [32768, 2048], P(('dp', 'expert')), may hold values from -24 to 24
- grad_out: bfloat16 [32768, 2048], P(('dp', 'expert')), may hold values from -6 to 6
- expert_ids: int32 [32768, 6], P(('dp', 'expert')), may hold values from 0 to 63, all different within a row
- route_weights: float32 [32768, 6], P(('dp', 'expert')), may hold values from 0.05 to 0.5
- w_gate: bfloat16 [16, 2048, 768], P('expert'), may hold values from -0.125 to 0.125
- w_up: bfloat16 [16, 2048, 768], P('expert'), may hold values from -0.125 to 0.125
- w_down: bfloat16 [16, 2048, 768], P('expert'), may hold values from -0.21875 to 0.21875
Outputs:
- mixed: bfloat16 [32768, 2048], P(('dp', 'expert'))
- grad_tokens: bfloat16 [32768, 2048], P(('dp', 'expert'))
- grad_route: float32 [32768, 6], P(('dp', 'expert'))
- grad_gate: float32 [16, 2048, 768], P('expert', 'dp')
- grad_up: float32 [16, 2048, 768], P('expert', 'dp')
- grad_down: float32 [16, 2048, 768], P('expert', 'dp')
The draws below stay inside these ranges and needn't reach their ends.
Inputs may be any that keep to these rules, and one draw needn't show every extreme that they name: `expert_ids`: each row names 6 different experts; only experts below 16 belong to this window.
All inputs are finite; a program needn't handle non-finite values.
Results may differ from the reference program's by a relative error of at most 0.033.
Values may be sent and summed in bfloat16 or wider, within the bound.
No kernel may reach another device: no remote copies, remote signals or barrier semaphores. Data moves between devices by JAX's collectives and lax.ppermute only.
A program may use at most 128 MiB of HBM per device.

```python
import functools
import jax
import jax.numpy as jnp
from jax import lax

D = 2048
ROUTED = 64
TOP = 6
FF_WIN = 768
TOK_DEV = 128
CAP = 24
EXPERTS = 16
TOKENS = 32768
N_DP = 16
N_EXPERT = 16


def spiked(values, rng, source, target, blocks, factor):
    def block_of(dim):
        return (jnp.arange(values.shape[dim]) // (values.shape[dim] // blocks)).reshape((-1,) + (1,) * (values.ndim - 1 - dim))

    first = jax.random.permutation(rng, blocks)[block_of(target)]
    second = (block_of(target) + blocks // 2) % blocks
    return jnp.where((block_of(source) == first) | (block_of(source) == second), factor * values, values)


def level_of(rng, dims, split, least, top_value):
    gain, own = 1.0, jax.random.fold_in(rng, 6)
    for axis_at, blocks in split:
        steps = jnp.exp(jax.random.uniform(jax.random.fold_in(own, axis_at), (blocks,), jnp.float32, least / len(split), top_value / len(split)))
        gain = gain * jnp.repeat(steps, dims[axis_at] // blocks).reshape([-1 if axis == axis_at else 1 for axis in range(len(dims))])
    return gain


def picks_of(key, rows, count, top, lift):
    ranking = jax.random.permutation(jax.random.fold_in(key, 1), count)
    pull = ranking
    for power in range(3):
        pull = pull * pull // count
    pull = pull * lift // count
    chance = jax.random.randint(jax.random.fold_in(key, 2), (rows, count), 0, 4096) + pull
    fixed_rows = jax.random.permutation(jax.random.fold_in(key, 3), rows)[jnp.arange(count) % rows]
    chance = jnp.where(jnp.arange(rows)[:, None] == fixed_rows[None, :], 1 << 14, chance)
    merit = chance * count + jnp.arange(count)
    return lax.top_k(merit.astype(jnp.int32), top)[1].astype(jnp.int32)


def noise(stream_key, shape, deviation, bound, shards=(), held_as=jnp.bfloat16):
    result = deviation * jax.random.normal(stream_key, shape, jnp.float32)
    if shards:
        result = result * level_of(stream_key, shape, shards, -0.22, 0.18)
    return jnp.clip(result, -bound, bound).astype(held_as)


def bell_draw_with(own_key, extent, scale, bound, shards, heavy, kind=jnp.bfloat16):
    array = scale * jax.random.normal(own_key, extent, jnp.float32)
    if shards:
        array = array * level_of(own_key, extent, shards, -0.22, 0.18)
    return jnp.clip(spiked(array, jax.random.fold_in(own_key, 3), *heavy), -bound, bound).astype(kind)


def setup_inputs(seed: int = 0) -> dict:
    keys = jax.random.split(jax.random.key(seed), 8)
    return {
        "tokens": bell_draw_with(keys[0], (TOKENS, D), 1.0, 24.0, ((0, 256),), (0, 1, 256, 6.0)),
        "grad_out": noise(keys[1], (TOKENS, D), 1.0, 6.0, ((0, 256),)),
        "expert_ids": picks_of(keys[2], TOKENS, ROUTED, TOP, 1536),
        "route_weights": jnp.clip(0.05 + 0.45 * jax.random.uniform(keys[3], (TOKENS, TOP), jnp.float32) ** level_of(keys[3], (TOKENS, TOP), ((0, 256),), -0.2, 0.2), 0.05, 0.5),
        "w_gate": noise(keys[4], (EXPERTS, D, FF_WIN), D ** -0.5, 0.125, ((0, 16),)),
        "w_up": noise(keys[5], (EXPERTS, D, FF_WIN), D ** -0.5, 0.125, ((0, 16),)),
        "w_down": noise(keys[6], (EXPERTS, D, FF_WIN), FF_WIN ** -0.5, 0.21875, ((0, 16),)),
    }


def slot_table(expert_ids, experts, capacity):
    pick_list = expert_ids.reshape(-1)
    expert_range = jnp.arange(experts, dtype=jnp.int32)
    matched = (pick_list[:, None] == expert_range[None, :]).astype(jnp.int32)
    earlier = jnp.cumsum(matched, axis=0) - matched
    position = jnp.sum(earlier * matched, axis=1)
    retained = (pick_list < experts) & (position < capacity)
    target = jnp.where(retained, pick_list * capacity + position, -1)
    return target.reshape(expert_ids.shape).astype(jnp.int32)


def slot_sources(target, route_weights, slot_total):
    slot_ids = jnp.arange(slot_total, dtype=jnp.int32)
    matches = target[None, :, :] == slot_ids[:, None, None]
    row_ids = jnp.arange(target.shape[0], dtype=jnp.int32)
    source = jnp.sum(jnp.where(matches, row_ids[None, :, None], 0), axis=(1, 2)).astype(jnp.int32)
    occupied = jnp.any(matches, axis=(1, 2))
    slot_weight = jnp.sum(jnp.where(matches, route_weights[None, :, :], 0.0), axis=(1, 2))
    return source, occupied, slot_weight


def dispatch_block(tokens, grad_out, source, occupied, slot_weight):
    picked_rows = tokens[source]
    picked_grads = grad_out[source].astype(jnp.float32)
    send_rows = jnp.where(occupied[:, None], picked_rows, jnp.zeros_like(picked_rows))
    send_grads = (jnp.where(occupied, slot_weight, 0.0)[:, None] * picked_grads).astype(jnp.bfloat16)
    return send_rows, send_grads


def combine_block(returned_out, returned_dx, grad_out, target, route_weights):
    kept = target >= 0
    safe = jnp.where(kept, target, 0).astype(jnp.int32)
    out_rows = returned_out[safe].astype(jnp.float32)
    dx_rows = returned_dx[safe].astype(jnp.float32)
    pick_weight = jnp.where(kept, route_weights, 0.0)
    mixed = jnp.sum(pick_weight[:, :, None] * out_rows, axis=1).astype(jnp.bfloat16)
    grad_tokens = jnp.sum(jnp.where(kept[:, :, None], dx_rows, 0.0), axis=1).astype(jnp.bfloat16)
    alignment = jnp.sum(out_rows * grad_out.astype(jnp.float32)[:, None, :], axis=2)
    grad_route = jnp.where(kept, alignment, 0.0)
    return mixed, grad_tokens, grad_route


def expert_rows(inputs, upstream, gate_w, up_w, down_w):
    contract_last = (((1,), (1,)), ((), ()))
    gate_pre = jnp.dot(inputs, gate_w, preferred_element_type=jnp.float32)
    up_pre = jnp.dot(inputs, up_w, preferred_element_type=jnp.float32)
    hidden = (jax.nn.silu(gate_pre) * up_pre).astype(jnp.bfloat16)
    expert_out = lax.dot_general(hidden, down_w, contract_last, preferred_element_type=jnp.float32).astype(jnp.bfloat16)
    d_hidden = jnp.dot(upstream, down_w, preferred_element_type=jnp.float32)
    sigmoid_gate = jax.nn.sigmoid(gate_pre)
    d_up = (d_hidden * gate_pre * sigmoid_gate).astype(jnp.bfloat16)
    d_gate = (d_hidden * up_pre * sigmoid_gate * (1.0 + gate_pre * (1.0 - sigmoid_gate))).astype(jnp.bfloat16)
    expert_dx = (lax.dot_general(d_gate, gate_w, contract_last, preferred_element_type=jnp.float32)
                 + lax.dot_general(d_up, up_w, contract_last, preferred_element_type=jnp.float32)).astype(jnp.bfloat16)
    return hidden, expert_out, d_gate, d_up, expert_dx


def reference(tokens, grad_out, expert_ids, route_weights, w_gate, w_up, w_down):
    block_count = N_DP * N_EXPERT
    slot_total = EXPERTS * CAP
    tok_blocks = tokens.reshape(block_count, TOK_DEV, D)
    grad_blocks = grad_out.reshape(block_count, TOK_DEV, D)
    ids_blocks = expert_ids.reshape(block_count, TOK_DEV, TOP)
    weight_blocks = route_weights.reshape(block_count, TOK_DEV, TOP)
    targets = jax.vmap(functools.partial(slot_table, experts=EXPERTS, capacity=CAP))(ids_blocks)
    source, occupied, slot_weight = jax.vmap(functools.partial(slot_sources, slot_total=slot_total))(targets, weight_blocks)
    send_rows, send_grads = jax.vmap(dispatch_block)(tok_blocks, grad_blocks, source, occupied, slot_weight)

    def by_expert(buffer):
        shaped = buffer.reshape(N_DP, N_EXPERT, EXPERTS, CAP, D).transpose(2, 0, 1, 3, 4)
        return shaped.reshape(EXPERTS, N_DP, N_EXPERT * CAP, D)

    first_dims = (((0,), (0,)), ((), ()))

    def expert_pass(bundle):
        rows_all, grads_all, gate_w, up_w, down_w = bundle

        def one_group(running, group_pair):
            inputs, upstream = group_pair
            hidden, expert_out, d_gate, d_up, expert_dx = expert_rows(inputs, upstream, gate_w, up_w, down_w)
            partial_value = jnp.stack([
                lax.dot_general(inputs, d_gate, first_dims, preferred_element_type=jnp.float32),
                lax.dot_general(inputs, d_up, first_dims, preferred_element_type=jnp.float32),
                lax.dot_general(upstream, hidden, first_dims, preferred_element_type=jnp.float32)])
            partial_value = partial_value.astype(jnp.bfloat16).astype(jnp.float32)
            return running + partial_value, (expert_out, expert_dx)

        initial = jnp.zeros((3, D, FF_WIN), jnp.float32)
        return lax.scan(one_group, initial, (rows_all, grads_all))

    grads, outputs = lax.map(expert_pass, (by_expert(send_rows), by_expert(send_grads), w_gate, w_up, w_down))
    out_all, dx_all = outputs

    def by_block(buffer):
        shaped = buffer.reshape(EXPERTS, N_DP, N_EXPERT, CAP, D).transpose(1, 2, 0, 3, 4)
        return shaped.reshape(block_count, slot_total, D)

    mixed, grad_tokens, grad_route = jax.vmap(combine_block)(by_block(out_all), by_block(dx_all), grad_blocks, targets, weight_blocks)
    return (mixed.reshape(TOKENS, D), grad_tokens.reshape(TOKENS, D), grad_route.reshape(TOKENS, TOP),
            grads[:, 0], grads[:, 1], grads[:, 2])
```

```python
import functools

import jax
import jax.numpy as jnp
from jax import lax
from jax.experimental import pallas as pl
from jax.experimental.pallas import tpu as pltpu
from jax.sharding import PartitionSpec as P

CAP = 24
EXPERTS = 16
SLOTS = EXPERTS * CAP
ROWS = 128
TOP = 6
D = 2048
FF = 768
RING = 4
MIB = 1024 * 1024
F32 = jnp.float32
BF16 = jnp.bfloat16
ALL = ("dp", "expert")


def ring_perm(axis):
    pairs = []
    for dp in range(16):
        x, z = divmod(dp, RING)
        for expert in range(16):
            step = 1 if expert % 2 == 0 else -1
            if axis == "x":
                to = ((x + step) % RING) * RING + z
            else:
                to = x * RING + (z + step) % RING
            pairs.append((dp * 16 + expert, to * 16 + expert))
    return pairs


def dot(a, b, contract):
    return lax.dot_general(a, b, ((contract[:1], contract[1:]), ((), ())), preferred_element_type=F32)


def place_kernel(ids_ref, weights_ref, tokens_ref, grads_ref, send_ref, target_ref):
    ids = ids_ref[...]
    weights = weights_ref[...]
    expert = lax.broadcasted_iota(jnp.int32, (EXPERTS, ROWS), 0)
    picked = jnp.zeros((EXPERTS, ROWS), F32)
    for k in range(TOP):
        picked = picked + jnp.where(ids[k : k + 1, :] == expert, 1.0, 0.0)
    earlier = lax.broadcasted_iota(jnp.int32, (ROWS, ROWS), 0) < lax.broadcasted_iota(
        jnp.int32, (ROWS, ROWS), 1
    )
    position = jnp.dot(
        picked.astype(BF16),
        jnp.where(earlier, 1.0, 0.0).astype(BF16),
        preferred_element_type=F32,
    )
    slot = lax.broadcasted_iota(jnp.int32, (SLOTS, ROWS), 0)
    chosen = jnp.zeros((SLOTS, ROWS), F32)
    scale = jnp.zeros((SLOTS, ROWS), F32)
    for k in range(TOP):
        pick = ids[k : k + 1, :]
        own = jnp.sum(jnp.where(pick == expert, position, 0.0), axis=0, keepdims=True)
        place = own.astype(jnp.int32)
        target = jnp.where((pick < EXPERTS) & (place < CAP), pick * CAP + place, -1)
        target_ref[k : k + 1, :] = target
        here = target == slot
        chosen = chosen + jnp.where(here, 1.0, 0.0)
        scale = scale + jnp.where(here, weights[k : k + 1, :], 0.0)
    chosen = chosen.astype(BF16)
    slot_scale = jnp.sum(scale, axis=1, keepdims=True)
    send_ref[:, :D] = jnp.dot(chosen, tokens_ref[...], preferred_element_type=F32).astype(BF16)
    send_ref[:, D:] = (
        slot_scale * jnp.dot(chosen, grads_ref[...], preferred_element_type=F32)
    ).astype(BF16)


def place(ids, weights, tokens, grads):
    return pl.pallas_call(
        place_kernel,
        out_shape=(
            jax.ShapeDtypeStruct((SLOTS, 2 * D), BF16),
            jax.ShapeDtypeStruct((TOP, ROWS), jnp.int32),
        ),
        compiler_params=pltpu.CompilerParams(vmem_limit_bytes=40 * MIB),
        cost_estimate=pl.CostEstimate(flops=4 * 10**8, bytes_accessed=5 * MIB, transcendentals=0),
        name="place_rows",
    )(ids, weights, tokens, grads)


def hidden_kernel(rows_ref, gate_ref, up_ref, down_ref, hidden_ref, d_gate_ref, d_up_ref):
    inputs = rows_ref[:, :D]
    gate_pre = jnp.dot(inputs, gate_ref[...], preferred_element_type=F32)
    up_pre = jnp.dot(inputs, up_ref[...], preferred_element_type=F32)
    d_hidden = jnp.dot(rows_ref[:, D:], down_ref[...], preferred_element_type=F32)
    sigmoid = jax.nn.sigmoid(gate_pre)
    silu = gate_pre * sigmoid
    hidden_ref[...] = (silu * up_pre).astype(BF16)
    d_up_ref[...] = (d_hidden * silu).astype(BF16)
    d_gate_ref[...] = (d_hidden * up_pre * sigmoid * (1.0 + gate_pre * (1.0 - sigmoid))).astype(BF16)


def hidden_pass(rows, gate_w, up_w, down_w):
    tile = 256
    weight = pl.BlockSpec((D, tile), lambda i: (0, i))
    out = pl.BlockSpec((SLOTS, tile), lambda i: (0, i))
    return pl.pallas_call(
        hidden_kernel,
        grid=(FF // tile,),
        in_specs=[pl.BlockSpec((SLOTS, 2 * D), lambda i: (0, 0)), weight, weight, weight],
        out_specs=[out] * 3,
        out_shape=[jax.ShapeDtypeStruct((SLOTS, FF), BF16)] * 3,
        compiler_params=pltpu.CompilerParams(vmem_limit_bytes=40 * MIB),
        cost_estimate=pl.CostEstimate(
            flops=6 * SLOTS * D * FF, bytes_accessed=14 * MIB, transcendentals=SLOTS * FF
        ),
        name="hidden_pass",
    )(rows, gate_w, up_w, down_w)


OUT_TILE = 512


def back_kernel(hidden_ref, d_gate_ref, d_up_ref, gate_ref, up_ref, down_ref, out_ref):
    out_ref[:, :OUT_TILE] = dot(hidden_ref[...], down_ref[...], (1, 1)).astype(BF16)
    out_ref[:, OUT_TILE:] = (
        dot(d_gate_ref[...], gate_ref[...], (1, 1)) + dot(d_up_ref[...], up_ref[...], (1, 1))
    ).astype(BF16)


def back_pass(hidden, d_gate, d_up, gate_w, up_w, down_w):
    act = pl.BlockSpec((SLOTS, FF), lambda i: (0, 0))
    weight = pl.BlockSpec((OUT_TILE, FF), lambda i: (i, 0))
    return pl.pallas_call(
        back_kernel,
        grid=(D // OUT_TILE,),
        in_specs=[act, act, act, weight, weight, weight],
        out_specs=pl.BlockSpec((SLOTS, 2 * OUT_TILE), lambda i: (0, i)),
        out_shape=jax.ShapeDtypeStruct((SLOTS, 2 * D), BF16),
        compiler_params=pltpu.CompilerParams(vmem_limit_bytes=40 * MIB),
        cost_estimate=pl.CostEstimate(
            flops=6 * SLOTS * D * FF, bytes_accessed=14 * MIB, transcendentals=0
        ),
        name="back_pass",
    )(hidden, d_gate, d_up, gate_w, up_w, down_w)


def partial_kernel(at_ref, lhs_ref, rhs_ref, *refs):
    total = dot(lhs_ref[...], rhs_ref[...], (0, 0))
    if len(refs) == 2:
        total = total + refs[0][...].astype(F32)
    refs[-1][...] = total.astype(BF16)


def partial_last_kernel(at_ref, lhs_ref, rhs_ref, got_ref, *out_refs):
    for i, out_ref in enumerate(out_refs):
        start = pl.multiple_of(at_ref[1 + i] * ROWS, ROWS)
        total = dot(lhs_ref[:, pl.ds(start, ROWS)], rhs_ref[...], (0, 0))
        total = total + got_ref[pl.ds(start, ROWS), :].astype(F32)
        out_ref[...] = total.astype(BF16)


def partial_sum(at, rows, half, grads, column, width, got, last):
    chunk = D // RING
    in_specs = [
        pl.BlockSpec((SLOTS, chunk), lambda i, at: (0, half * RING + at[0])),
        pl.BlockSpec((SLOTS, width), lambda i, at: (0, column)),
    ]
    args = [rows, grads]
    whole = pl.BlockSpec((chunk, width), lambda i, at: (0, 0))
    if got is not None:
        in_specs.append(whole)
        args.append(got)
    if last:
        out_specs = [pl.BlockSpec((ROWS, width), lambda i, at: (0, 0))] * RING
        out_shape = [jax.ShapeDtypeStruct((ROWS, width), BF16)] * RING
    else:
        out_specs = whole
        out_shape = jax.ShapeDtypeStruct((chunk, width), BF16)
    return pl.pallas_call(
        partial_last_kernel if last else partial_kernel,
        grid_spec=pltpu.PrefetchScalarGridSpec(
            num_scalar_prefetch=1, grid=(1,), in_specs=in_specs, out_specs=out_specs
        ),
        out_shape=out_shape,
        compiler_params=pltpu.CompilerParams(vmem_limit_bytes=24 * MIB),
        cost_estimate=pl.CostEstimate(
            flops=2 * SLOTS * chunk * width, bytes_accessed=3 * MIB, transcendentals=0
        ),
        name="partial_last" if last else "partial_sum",
    )(at, *args)


def combine_kernel(target_ref, weights_ref, back_ref, grads_ref, mixed_ref, d_tokens_ref, d_route_ref):
    weights = weights_ref[...]
    slot = lax.broadcasted_iota(jnp.int32, (SLOTS, ROWS), 0)
    align = jnp.zeros((SLOTS, ROWS), F32)
    tiles = D // OUT_TILE
    for i in range(tiles):
        out = back_ref[:, 2 * i * OUT_TILE : (2 * i + 1) * OUT_TILE]
        align = align + dot(out, grads_ref[:, i * OUT_TILE : (i + 1) * OUT_TILE], (1, 1))
    chosen = jnp.zeros((SLOTS, ROWS), F32)
    scale = jnp.zeros((SLOTS, ROWS), F32)
    for k in range(TOP):
        here = target_ref[k : k + 1, :] == slot
        chosen = chosen + jnp.where(here, 1.0, 0.0)
        scale = scale + jnp.where(here, weights[k : k + 1, :], 0.0)
        d_route_ref[k : k + 1, :] = jnp.sum(jnp.where(here, align, 0.0), axis=0, keepdims=True)
    chosen = chosen.astype(BF16)
    high = scale.astype(BF16)
    low = (scale - high.astype(F32)).astype(BF16)
    for i in range(tiles):
        out = back_ref[:, 2 * i * OUT_TILE : (2 * i + 1) * OUT_TILE]
        d_in = back_ref[:, (2 * i + 1) * OUT_TILE : (2 * i + 2) * OUT_TILE]
        at = slice(i * OUT_TILE, (i + 1) * OUT_TILE)
        mixed_ref[:, at] = (dot(high, out, (0, 0)) + dot(low, out, (0, 0))).astype(BF16)
        d_tokens_ref[:, at] = dot(chosen, d_in, (0, 0)).astype(BF16)


def combine(target, weights, back, grads):
    return pl.pallas_call(
        combine_kernel,
        out_shape=(
            jax.ShapeDtypeStruct((ROWS, D), BF16),
            jax.ShapeDtypeStruct((ROWS, D), BF16),
            jax.ShapeDtypeStruct((TOP, ROWS), F32),
        ),
        compiler_params=pltpu.CompilerParams(vmem_limit_bytes=40 * MIB),
        cost_estimate=pl.CostEstimate(flops=10**9, bytes_accessed=6 * MIB, transcendentals=0),
        name="combine_rows",
    )(target, weights, back, grads)


def on_device(tokens, grad_out, expert_ids, route_weights, w_gate, w_up, w_down):
    x, z = lax.axis_index("dp") // RING, lax.axis_index("dp") % RING
    step = 1 - 2 * (lax.axis_index("expert") % 2)
    x_at = [(x - (i + 1) * step) % RING for i in range(RING)]
    z_at = [(z - (i + 1) * step) % RING for i in range(RING)]
    order = [jnp.stack([at, *z_at]).astype(jnp.int32) for at in x_at]
    x_perm, z_perm = ring_perm("x"), ring_perm("z")
    gate_w, up_w, down_w = w_gate[0], w_up[0], w_down[0]
    ids, weights = expert_ids.T, route_weights.T

    def exchange(buffer):
        buffer = buffer.reshape(EXPERTS, CAP, 2 * D)
        buffer = lax.all_to_all(buffer, "expert", split_axis=0, concat_axis=0, tiled=True)
        return buffer.reshape(SLOTS, 2 * D)

    send, target = place(ids, weights, tokens, grad_out)
    rows = exchange(send)
    hidden, d_gate, d_up = hidden_pass(rows, gate_w, up_w, down_w)

    def x_ring(half, grads, column, width):
        got = None
        for i in range(RING):
            total = partial_sum(order[i], rows, half, grads, column, width, got, i == RING - 1)
            if i < RING - 1:
                got = lax.ppermute(total, ALL, x_perm)
        return total

    def z_ring(parts):
        total = parts[0]
        for i in range(1, RING):
            got = lax.ppermute(total, ALL, z_perm).astype(F32)
            total = parts[i].astype(F32) + got
            if i < RING - 1:
                total = total.astype(BF16)
        return total

    grad_down = z_ring(x_ring(1, hidden, 0, FF))
    grad_gate = z_ring(x_ring(0, d_gate, 0, FF))
    back = exchange(back_pass(hidden, d_gate, d_up, gate_w, up_w, down_w))
    grad_up = jnp.concatenate(
        [z_ring(x_ring(0, d_up, i, FF // 2)) for i in range(2)], axis=1
    )
    mixed, d_tokens, d_route = combine(target, weights, back, grad_out)
    return (mixed, d_tokens, d_route.T, grad_gate[None], grad_up[None], grad_down[None])


def solution(mesh):
    by_device = P(("dp", "expert"), None)
    by_expert = P("expert", None, None)
    by_row = P("expert", "dp", None)
    return jax.shard_map(
        on_device,
        mesh=mesh,
        in_specs=(by_device,) * 4 + (by_expert,) * 3,
        out_specs=(by_device,) * 3 + (by_row,) * 3,
        check_vma=False,
    )
```

```python
import jax
import jax.numpy as jnp
from jax import lax
from jax.experimental import pallas as pl
from jax.experimental.pallas import tpu as pltpu
from jax.sharding import PartitionSpec as P

CAP = 24
EXPERTS = 16
SLOTS = EXPERTS * CAP
ROWS = 128
TOP = 6
D = 2048
FF = 768
RING = 4
MIB = 1024 * 1024
LONG = pl.CostEstimate(flops=10**10, bytes_accessed=MIB, transcendentals=0)
STEP = pl.CostEstimate(flops=10**10, bytes_accessed=1, transcendentals=0)
SMALL = pl.CostEstimate(flops=1, bytes_accessed=1, transcendentals=0)
F32 = jnp.float32
BF16 = jnp.bfloat16
ALL = ("dp", "expert")
ORDER = (
    "first gate",
    "run back",
    "all up",
    "rest gate",
    "second gate",
    "all down",
    "third gate",
    "second up",
    "fourth gate",
    "third up",
    "second down",
    "run combine",
    "fifth gate",
    "fourth up",
    "third down",
    "fifth up",
    "fourth down",
    "fifth down",
)


def partners(core, at):
    beside, across = at ^ 1, RING - 1 - at
    first, second = (beside, across) if core == 0 else (across, beside)
    return first, second, (at + 2) % RING


def pairs_of(axis, stage):
    pairs = []
    for dp in range(RING * RING):
        x, z = divmod(dp, RING)
        for expert in range(EXPERTS):
            if axis == "x":
                to = partners(expert % 2, x)[stage] * RING + z
            else:
                to = x * RING + partners(expert % 2, z)[stage]
            pairs.append((dp * EXPERTS + expert, to * EXPERTS + expert))
    return pairs


def dot(a, b, contract):
    return lax.dot_general(a, b, ((contract[:1], contract[1:]), ((), ())), preferred_element_type=F32)


def place_kernel(at_ref, ids_ref, weights_ref, tokens_ref, grads_ref, send_ref, target_ref):
    ids = ids_ref[...]
    weights = weights_ref[...]
    expert = lax.broadcasted_iota(jnp.int32, (EXPERTS, ROWS), 0)
    picked = jnp.zeros((EXPERTS, ROWS), F32)
    for k in range(TOP):
        picked = picked + jnp.where(ids[k : k + 1, :] == expert, 1.0, 0.0)
    earlier = lax.broadcasted_iota(jnp.int32, (ROWS, ROWS), 0) < lax.broadcasted_iota(
        jnp.int32, (ROWS, ROWS), 1
    )
    position = jnp.dot(
        picked.astype(BF16),
        jnp.where(earlier, 1.0, 0.0).astype(BF16),
        preferred_element_type=F32,
    )
    slot = lax.broadcasted_iota(jnp.int32, (SLOTS, ROWS), 0)
    chosen = jnp.zeros((SLOTS, ROWS), F32)
    scale = jnp.zeros((SLOTS, ROWS), F32)
    for k in range(TOP):
        pick = ids[k : k + 1, :]
        own = jnp.sum(jnp.where(pick == expert, position, 0.0), axis=0, keepdims=True)
        place = own.astype(jnp.int32)
        target = jnp.where((pick < EXPERTS) & (place < CAP), pick * CAP + place, -1)
        target_ref[k : k + 1, :] = target
        here = target == slot
        chosen = chosen + jnp.where(here, 1.0, 0.0)
        scale = scale + jnp.where(here, weights[k : k + 1, :], 0.0)
    chosen = chosen.astype(BF16)
    slot_scale = jnp.sum(scale, axis=1, keepdims=True)
    send_ref[:, :D] = jnp.dot(chosen, tokens_ref[...], preferred_element_type=F32).astype(BF16)
    send_ref[:, D:] = (
        slot_scale * jnp.dot(chosen, grads_ref[...], preferred_element_type=F32)
    ).astype(BF16)


def place(at, ids, weights, tokens, grads):
    whole = pl.BlockSpec(memory_space=pltpu.VMEM)
    return pl.pallas_call(
        place_kernel,
        in_specs=[pl.BlockSpec(memory_space=pltpu.SMEM)] + [whole] * 4,
        out_shape=(
            jax.ShapeDtypeStruct((SLOTS, 2 * D), BF16),
            jax.ShapeDtypeStruct((TOP, ROWS), jnp.int32),
        ),
        compiler_params=pltpu.CompilerParams(vmem_limit_bytes=20 * MIB),
        cost_estimate=pl.CostEstimate(flops=4 * 10**10, bytes_accessed=5 * MIB, transcendentals=0),
        name="place_rows",
    )(at, ids, weights, tokens, grads)


def hidden_kernel(rows_ref, gate_ref, up_ref, down_ref, hidden_ref, d_gate_ref, d_up_ref):
    inputs = rows_ref[:, :D]
    gate_pre = jnp.dot(inputs, gate_ref[...], preferred_element_type=F32)
    up_pre = jnp.dot(inputs, up_ref[...], preferred_element_type=F32)
    d_hidden = jnp.dot(rows_ref[:, D:], down_ref[...], preferred_element_type=F32)
    sigmoid = jax.nn.sigmoid(gate_pre)
    silu = gate_pre * sigmoid
    hidden_ref[...] = (silu * up_pre).astype(BF16)
    d_up_ref[...] = (d_hidden * silu).astype(BF16)
    d_gate_ref[...] = (d_hidden * up_pre * sigmoid * (1.0 + gate_pre * (1.0 - sigmoid))).astype(BF16)


def hidden_pass(rows, gate_w, up_w, down_w):
    tile = 256
    weight = pl.BlockSpec((D, tile), lambda i: (0, i))
    out = pl.BlockSpec((SLOTS, tile), lambda i: (0, i))
    return pl.pallas_call(
        hidden_kernel,
        grid=(FF // tile,),
        in_specs=[pl.BlockSpec((SLOTS, 2 * D), lambda i: (0, 0)), weight, weight, weight],
        out_specs=[out] * 3,
        out_shape=[jax.ShapeDtypeStruct((SLOTS, FF), BF16)] * 3,
        compiler_params=pltpu.CompilerParams(vmem_limit_bytes=20 * MIB),
        cost_estimate=SMALL,
        name="hidden_pass",
    )(rows, gate_w, up_w, down_w)


OUT_TILE = 512
CHUNK = D // RING
ANY = pl.BlockSpec(memory_space=pl.ANY)
TOKEN = jax.ShapeDtypeStruct((8, 128), jnp.int32)


def at_zero(*shape):
    return pl.BlockSpec(shape, lambda *_: (0,) * len(shape))


def emit(token_ref):
    token_ref[...] = jnp.zeros(token_ref.shape, token_ref.dtype)


def back_kernel(
    hidden_ref, d_gate_ref, d_up_ref, gate_ref, up_ref, down_ref, after_ref, out_ref, token_ref
):
    out_ref[:, :OUT_TILE] = dot(hidden_ref[...], down_ref[...], (1, 1)).astype(BF16)
    out_ref[:, OUT_TILE:] = (
        dot(d_gate_ref[...], gate_ref[...], (1, 1)) + dot(d_up_ref[...], up_ref[...], (1, 1))
    ).astype(BF16)
    emit(token_ref)


def back_pass(hidden, d_gate, d_up, gate_w, up_w, down_w, after):
    act = at_zero(SLOTS, FF)
    weight = pl.BlockSpec((OUT_TILE, FF), lambda i: (i, 0))
    return pl.pallas_call(
        back_kernel,
        grid=(D // OUT_TILE,),
        in_specs=[act, act, act, weight, weight, weight, ANY],
        out_specs=[pl.BlockSpec((SLOTS, 2 * OUT_TILE), lambda i: (0, i)), at_zero(8, 128)],
        out_shape=[jax.ShapeDtypeStruct((SLOTS, 2 * D), BF16), TOKEN],
        compiler_params=pltpu.CompilerParams(vmem_limit_bytes=20 * MIB),
        cost_estimate=SMALL,
        name="back_pass",
    )(hidden, d_gate, d_up, gate_w, up_w, down_w, after)


def partial_kernel(at_ref, lhs_ref, rhs_ref, after_ref, *refs):
    value = dot(lhs_ref[...], rhs_ref[...], (0, 0)).astype(BF16)
    *out_refs, token_ref = refs
    for i, out_ref in enumerate(out_refs):
        if len(out_refs) == 1:
            out_ref[...] = value
        else:

            @pl.when(pl.program_id(0) // 2 == i)
            def _():
                out_ref[...] = value

    emit(token_ref)


def partial(at, rows, side, first, count, grads, column, width, after):
    def out_spec(i):
        return pl.BlockSpec(
            (CHUNK, width), lambda s, at: (jnp.clip(s - 2 * i, 0, 1) if count > 2 else s, 0)
        )

    outs = count // 2
    return pl.pallas_call(
        partial_kernel,
        grid_spec=pltpu.PrefetchScalarGridSpec(
            num_scalar_prefetch=1,
            grid=(count,),
            in_specs=[
                pl.BlockSpec((SLOTS, CHUNK), lambda s, at: (0, side * RING + at[first + s])),
                pl.BlockSpec((SLOTS, width), lambda s, at: (0, column)),
                ANY,
            ],
            out_specs=[out_spec(i) for i in range(outs)] + [at_zero(8, 128)],
        ),
        out_shape=[jax.ShapeDtypeStruct((2 * CHUNK, width), BF16)] * outs + [TOKEN],
        compiler_params=pltpu.CompilerParams(vmem_limit_bytes=12 * MIB),
        cost_estimate=SMALL,
        name="partial",
    )(at, rows, grads, after)


def split_kernel(own_ref, next_ref, got_next_ref, got_own_ref, after_ref, send_ref, keep_ref, token_ref):
    send_ref[...] = (next_ref[...].astype(F32) + got_next_ref[...].astype(F32)).astype(BF16)
    keep_ref[...] = (own_ref[...].astype(F32) + got_own_ref[...].astype(F32)).astype(BF16)
    emit(token_ref)


def split_sum(rows, own, next_, got, after):
    width = got.shape[1]

    def block(i):
        return pl.BlockSpec((rows, width), lambda s: (i, 0))

    out = jax.ShapeDtypeStruct((rows, width), BF16)
    return pl.pallas_call(
        split_kernel,
        grid=(1,),
        in_specs=[block(own[1]), block(next_[1]), block(0), block(1), ANY],
        out_specs=[block(0), block(0), at_zero(8, 128)],
        out_shape=[out, out, TOKEN],
        compiler_params=pltpu.CompilerParams(vmem_limit_bytes=16 * MIB),
        cost_estimate=STEP,
        name="split_sum",
    )(own[0], next_[0], got, got, after)


def third_kernel(at_ref, keep_ref, got_ref, after_ref, far_near_ref, next_own_ref, token_ref):
    for i in range(RING):
        rows = pl.ds(pl.multiple_of(at_ref[RING + i] * ROWS, ROWS), ROWS)
        total = (keep_ref[rows, :].astype(F32) + got_ref[rows, :].astype(F32)).astype(BF16)
        out_ref = far_near_ref if i < 2 else next_own_ref
        out_ref[i % 2 * ROWS : (i % 2 + 1) * ROWS, :] = total
    emit(token_ref)


def third_sum(at, keep, got, after, cost):
    width = keep.shape[1]
    return pl.pallas_call(
        third_kernel,
        grid_spec=pltpu.PrefetchScalarGridSpec(
            num_scalar_prefetch=1,
            grid=(1,),
            in_specs=[at_zero(CHUNK, width), at_zero(CHUNK, width), ANY],
            out_specs=[at_zero(2 * ROWS, width)] * 2 + [at_zero(8, 128)],
        ),
        out_shape=[jax.ShapeDtypeStruct((2 * ROWS, width), BF16)] * 2 + [TOKEN],
        compiler_params=pltpu.CompilerParams(vmem_limit_bytes=12 * MIB),
        cost_estimate=cost,
        name="third_sum",
    )(at, keep, got, after)


def fifth_kernel(keep_ref, got_ref, after_ref, out_ref, token_ref):
    out_ref[...] = keep_ref[...].astype(F32) + got_ref[...].astype(F32)
    emit(token_ref)


def fifth_sum(keep, got, after):
    width = keep.shape[1]
    block = at_zero(ROWS, width)
    return pl.pallas_call(
        fifth_kernel,
        grid=(1,),
        in_specs=[block, block, ANY],
        out_specs=[block, at_zero(8, 128)],
        out_shape=[jax.ShapeDtypeStruct((ROWS, width), F32), TOKEN],
        compiler_params=pltpu.CompilerParams(vmem_limit_bytes=4 * MIB),
        cost_estimate=STEP,
        name="fifth_sum",
    )(keep, got, after)


def combine_kernel(target_ref, weights_ref, back_ref, grads_ref, after_ref, mixed_ref, d_tokens_ref, d_route_ref, token_ref
):
    emit(token_ref)
    weights = weights_ref[...]
    slot = lax.broadcasted_iota(jnp.int32, (SLOTS, ROWS), 0)
    align = jnp.zeros((SLOTS, ROWS), F32)
    tiles = D // OUT_TILE
    for i in range(tiles):
        out = back_ref[:, 2 * i * OUT_TILE : (2 * i + 1) * OUT_TILE]
        align = align + dot(out, grads_ref[:, i * OUT_TILE : (i + 1) * OUT_TILE], (1, 1))
    chosen = jnp.zeros((SLOTS, ROWS), F32)
    scale = jnp.zeros((SLOTS, ROWS), F32)
    for k in range(TOP):
        here = target_ref[k : k + 1, :] == slot
        chosen = chosen + jnp.where(here, 1.0, 0.0)
        scale = scale + jnp.where(here, weights[k : k + 1, :], 0.0)
        d_route_ref[k : k + 1, :] = jnp.sum(jnp.where(here, align, 0.0), axis=0, keepdims=True)
    chosen = chosen.astype(BF16)
    high = scale.astype(BF16)
    low = (scale - high.astype(F32)).astype(BF16)
    for i in range(tiles):
        out = back_ref[:, 2 * i * OUT_TILE : (2 * i + 1) * OUT_TILE]
        d_in = back_ref[:, (2 * i + 1) * OUT_TILE : (2 * i + 2) * OUT_TILE]
        at = slice(i * OUT_TILE, (i + 1) * OUT_TILE)
        mixed_ref[:, at] = (dot(high, out, (0, 0)) + dot(low, out, (0, 0))).astype(BF16)
        d_tokens_ref[:, at] = dot(chosen, d_in, (0, 0)).astype(BF16)


def combine(target, weights, back, grads, after):
    whole = pl.BlockSpec(memory_space=pltpu.VMEM)
    return pl.pallas_call(
        combine_kernel,
        in_specs=[whole] * 4 + [ANY],
        out_shape=(
            jax.ShapeDtypeStruct((ROWS, D), BF16),
            jax.ShapeDtypeStruct((ROWS, D), BF16),
            jax.ShapeDtypeStruct((TOP, ROWS), F32),
            TOKEN,
        ),
        compiler_params=pltpu.CompilerParams(vmem_limit_bytes=20 * MIB),
        cost_estimate=SMALL,
        name="combine_rows",
    )(target, weights, back, grads, after)


def on_device(tokens, grad_out, expert_ids, route_weights, w_gate, w_up, w_down):
    x, z = lax.axis_index("dp") // RING, lax.axis_index("dp") % RING
    core = lax.axis_index("expert") % 2

    def chunk_order(at):
        beside, across = at ^ 1, RING - 1 - at
        first = jnp.where(core == 0, beside, across)
        second = jnp.where(core == 0, across, beside)
        return [(at + 2) % RING, first, second, at]

    at = jnp.stack(chunk_order(x) + chunk_order(z)).astype(jnp.int32)
    gate_w, up_w, down_w = w_gate[0], w_up[0], w_down[0]
    ids, weights = expert_ids.T, route_weights.T

    def exchange(buffer):
        buffer = buffer.reshape(EXPERTS, CAP, 2 * D)
        buffer = lax.all_to_all(buffer, "expert", split_axis=0, concat_axis=0, tiled=True)
        return buffer.reshape(SLOTS, 2 * D)

    def send_on(array, axis, stage):
        return lax.ppermute(array, ALL, pairs_of(axis, stage))

    send, target = place(at, ids, weights, tokens, grad_out)
    rows = exchange(send)
    hidden, d_gate, d_up = hidden_pass(rows, gate_w, up_w, down_w)

    factors = {"gate": (0, d_gate), "up": (0, d_up), "down": (1, hidden)}
    got, sums, grads = {}, {}, {}
    token = target
    back = None
    for step in ORDER:
        kind, name = step.split()
        if kind in ("first", "rest", "all"):
            side, factor = factors[name]
            start, count = {"first": (0, 2), "rest": (2, 2), "all": (0, 4)}[kind]
            *made, token = partial(at, rows, side, start, count, factor, 0, FF, token)
            if kind != "first":
                sums[name] = made[-1]
            if kind != "rest":
                got[name] = send_on(made[0], "x", 0)
        elif kind == "second":
            both = sums[name]
            send, sums[name], token = split_sum(CHUNK, (both, 1), (both, 0), got[name], token)
            got[name] = send_on(send, "x", 1)
        elif kind == "third":
            cost = LONG if name == "gate" else STEP
            send, sums[name], token = third_sum(at, sums[name], got[name], token, cost)
            got[name] = send_on(send, "z", 0)
        elif kind == "fourth":
            both = sums[name]
            send, sums[name], token = split_sum(ROWS, (both, 1), (both, 0), got[name], token)
            got[name] = send_on(send, "z", 1)
        elif kind == "fifth":
            total, token = fifth_sum(sums[name], got[name], token)
            grads[name] = total[None]
        elif name == "back":
            back, token = back_pass(hidden, d_gate, d_up, gate_w, up_w, down_w, token)
            back = exchange(back)
        else:
            mixed, d_tokens, d_route, token = combine(target, weights, back, grad_out, token)
    return (mixed, d_tokens, d_route.T) + tuple(grads[name] for name in ("gate", "up", "down"))


def solution(mesh):
    by_device = P(("dp", "expert"), None)
    by_expert = P("expert", None, None)
    by_row = P("expert", "dp", None)
    return jax.shard_map(
        on_device,
        mesh=mesh,
        in_specs=(by_device,) * 4 + (by_expert,) * 3,
        out_specs=(by_device,) * 3 + (by_row,) * 3,
        check_vma=False,
    )
```

```python
import jax
import jax.numpy as jnp
from jax import lax
from jax.experimental import pallas as pl
from jax.experimental.pallas import tpu as pltpu
from jax.sharding import PartitionSpec as P

CAP = 24
EXPERTS = 16
SLOTS = EXPERTS * CAP
ROWS = 128
TOP = 6
D = 2048
FF = 768
RING = 4
MIB = 1024 * 1024
LONG = pl.CostEstimate(flops=6 * 10**9, bytes_accessed=MIB, transcendentals=0)
STEP = pl.CostEstimate(flops=6 * 10**9, bytes_accessed=1, transcendentals=0)
SMALL = pl.CostEstimate(flops=1, bytes_accessed=1, transcendentals=0)
F32 = jnp.float32
BF16 = jnp.bfloat16
ALL = ("dp", "expert")
ORDER = (
    "first gate",
    "run back",
    "all up",
    "rest gate",
    "second gate",
    "all down",
    "third gate",
    "second up",
    "fourth gate",
    "third up",
    "second down",
    "fifth gate",
    "fourth up",
    "third down",
    "run combine",
    "fifth up",
    "fourth down",
    "fifth down",
)


def partners(core, at):
    beside, across = at ^ 1, RING - 1 - at
    first, second = (beside, across) if core == 0 else (across, beside)
    return first, second, (at + 2) % RING


def pairs_of(axis, stage):
    pairs = []
    for dp in range(RING * RING):
        x, z = divmod(dp, RING)
        for expert in range(EXPERTS):
            if axis == "x":
                to = partners(expert % 2, x)[stage] * RING + z
            else:
                to = x * RING + partners(expert % 2, z)[stage]
            pairs.append((dp * EXPERTS + expert, to * EXPERTS + expert))
    return pairs


def dot(a, b, contract):
    return lax.dot_general(a, b, ((contract[:1], contract[1:]), ((), ())), preferred_element_type=F32)


def place_kernel(at_ref, ids_ref, weights_ref, tokens_ref, grads_ref, send_ref, target_ref):
    ids = ids_ref[...]
    weights = weights_ref[...]
    expert = lax.broadcasted_iota(jnp.int32, (EXPERTS, ROWS), 0)
    picked = jnp.zeros((EXPERTS, ROWS), F32)
    for k in range(TOP):
        picked = picked + jnp.where(ids[k : k + 1, :] == expert, 1.0, 0.0)
    earlier = lax.broadcasted_iota(jnp.int32, (ROWS, ROWS), 0) < lax.broadcasted_iota(
        jnp.int32, (ROWS, ROWS), 1
    )
    position = jnp.dot(
        picked.astype(BF16),
        jnp.where(earlier, 1.0, 0.0).astype(BF16),
        preferred_element_type=F32,
    )
    slot = lax.broadcasted_iota(jnp.int32, (SLOTS, ROWS), 0)
    chosen = jnp.zeros((SLOTS, ROWS), F32)
    scale = jnp.zeros((SLOTS, ROWS), F32)
    for k in range(TOP):
        pick = ids[k : k + 1, :]
        own = jnp.sum(jnp.where(pick == expert, position, 0.0), axis=0, keepdims=True)
        place = own.astype(jnp.int32)
        target = jnp.where((pick < EXPERTS) & (place < CAP), pick * CAP + place, -1)
        target_ref[k : k + 1, :] = target
        here = target == slot
        chosen = chosen + jnp.where(here, 1.0, 0.0)
        scale = scale + jnp.where(here, weights[k : k + 1, :], 0.0)
    chosen = chosen.astype(BF16)
    slot_scale = jnp.sum(scale, axis=1, keepdims=True)
    send_ref[:, :D] = jnp.dot(chosen, tokens_ref[...], preferred_element_type=F32).astype(BF16)
    send_ref[:, D:] = (
        slot_scale * jnp.dot(chosen, grads_ref[...], preferred_element_type=F32)
    ).astype(BF16)


def place(at, ids, weights, tokens, grads):
    whole = pl.BlockSpec(memory_space=pltpu.VMEM)
    return pl.pallas_call(
        place_kernel,
        in_specs=[pl.BlockSpec(memory_space=pltpu.SMEM)] + [whole] * 4,
        out_shape=(
            jax.ShapeDtypeStruct((SLOTS, 2 * D), BF16),
            jax.ShapeDtypeStruct((TOP, ROWS), jnp.int32),
        ),
        compiler_params=pltpu.CompilerParams(vmem_limit_bytes=20 * MIB),
        cost_estimate=pl.CostEstimate(flops=4 * 10**10, bytes_accessed=5 * MIB, transcendentals=0),
        name="place_rows",
    )(at, ids, weights, tokens, grads)


def hidden_kernel(rows_ref, gate_ref, up_ref, down_ref, hidden_ref, d_gate_ref, d_up_ref):
    inputs = rows_ref[:, :D]
    gate_pre = jnp.dot(inputs, gate_ref[...], preferred_element_type=F32)
    up_pre = jnp.dot(inputs, up_ref[...], preferred_element_type=F32)
    d_hidden = jnp.dot(rows_ref[:, D:], down_ref[...], preferred_element_type=F32)
    sigmoid = jax.nn.sigmoid(gate_pre)
    silu = gate_pre * sigmoid
    hidden_ref[...] = (silu * up_pre).astype(BF16)
    d_up_ref[...] = (d_hidden * silu).astype(BF16)
    d_gate_ref[...] = (d_hidden * up_pre * sigmoid * (1.0 + gate_pre * (1.0 - sigmoid))).astype(BF16)


def hidden_pass(rows, gate_w, up_w, down_w):
    tile = 256
    weight = pl.BlockSpec((D, tile), lambda i: (0, i))
    out = pl.BlockSpec((SLOTS, tile), lambda i: (0, i))
    return pl.pallas_call(
        hidden_kernel,
        grid=(FF // tile,),
        in_specs=[pl.BlockSpec((SLOTS, 2 * D), lambda i: (0, 0)), weight, weight, weight],
        out_specs=[out] * 3,
        out_shape=[jax.ShapeDtypeStruct((SLOTS, FF), BF16)] * 3,
        compiler_params=pltpu.CompilerParams(vmem_limit_bytes=20 * MIB),
        cost_estimate=SMALL,
        name="hidden_pass",
    )(rows, gate_w, up_w, down_w)


OUT_TILE = 512
CHUNK = D // RING
ANY = pl.BlockSpec(memory_space=pl.ANY)
TOKEN = jax.ShapeDtypeStruct((8, 128), jnp.int32)


def at_zero(*shape):
    return pl.BlockSpec(shape, lambda *_: (0,) * len(shape))


def emit(token_ref):
    token_ref[...] = jnp.zeros(token_ref.shape, token_ref.dtype)


def back_kernel(
    hidden_ref, d_gate_ref, d_up_ref, gate_ref, up_ref, down_ref, after_ref, out_ref, token_ref
):
    out_ref[:, :OUT_TILE] = dot(hidden_ref[...], down_ref[...], (1, 1)).astype(BF16)
    out_ref[:, OUT_TILE:] = (
        dot(d_gate_ref[...], gate_ref[...], (1, 1)) + dot(d_up_ref[...], up_ref[...], (1, 1))
    ).astype(BF16)
    emit(token_ref)


def back_pass(hidden, d_gate, d_up, gate_w, up_w, down_w, after):
    act = at_zero(SLOTS, FF)
    weight = pl.BlockSpec((OUT_TILE, FF), lambda i: (i, 0))
    return pl.pallas_call(
        back_kernel,
        grid=(D // OUT_TILE,),
        in_specs=[act, act, act, weight, weight, weight, ANY],
        out_specs=[pl.BlockSpec((SLOTS, 2 * OUT_TILE), lambda i: (0, i)), at_zero(8, 128)],
        out_shape=[jax.ShapeDtypeStruct((SLOTS, 2 * D), BF16), TOKEN],
        compiler_params=pltpu.CompilerParams(vmem_limit_bytes=20 * MIB),
        cost_estimate=SMALL,
        name="back_pass",
    )(hidden, d_gate, d_up, gate_w, up_w, down_w, after)


def partial_kernel(at_ref, lhs_ref, rhs_ref, after_ref, *refs):
    value = dot(lhs_ref[...], rhs_ref[...], (0, 0)).astype(BF16)
    *out_refs, token_ref = refs
    for i, out_ref in enumerate(out_refs):
        if len(out_refs) == 1:
            out_ref[...] = value
        else:

            @pl.when(pl.program_id(0) // 2 == i)
            def _():
                out_ref[...] = value

    emit(token_ref)


def partial(at, rows, side, first, count, grads, column, width, after):
    def out_spec(i):
        return pl.BlockSpec(
            (CHUNK, width), lambda s, at: (jnp.clip(s - 2 * i, 0, 1) if count > 2 else s, 0)
        )

    outs = count // 2
    return pl.pallas_call(
        partial_kernel,
        grid_spec=pltpu.PrefetchScalarGridSpec(
            num_scalar_prefetch=1,
            grid=(count,),
            in_specs=[
                pl.BlockSpec((SLOTS, CHUNK), lambda s, at: (0, side * RING + at[first + s])),
                pl.BlockSpec((SLOTS, width), lambda s, at: (0, column)),
                ANY,
            ],
            out_specs=[out_spec(i) for i in range(outs)] + [at_zero(8, 128)],
        ),
        out_shape=[jax.ShapeDtypeStruct((2 * CHUNK, width), BF16)] * outs + [TOKEN],
        compiler_params=pltpu.CompilerParams(vmem_limit_bytes=12 * MIB),
        cost_estimate=SMALL,
        name="partial",
    )(at, rows, grads, after)


def split_kernel(own_ref, next_ref, got_next_ref, got_own_ref, after_ref, send_ref, keep_ref, token_ref):
    send_ref[...] = (next_ref[...].astype(F32) + got_next_ref[...].astype(F32)).astype(BF16)
    keep_ref[...] = (own_ref[...].astype(F32) + got_own_ref[...].astype(F32)).astype(BF16)
    emit(token_ref)


def split_sum(rows, own, next_, got, after):
    width = got.shape[1]

    def block(i):
        return pl.BlockSpec((rows, width), lambda s: (i, 0))

    out = jax.ShapeDtypeStruct((rows, width), BF16)
    return pl.pallas_call(
        split_kernel,
        grid=(1,),
        in_specs=[block(own[1]), block(next_[1]), block(0), block(1), ANY],
        out_specs=[block(0), block(0), at_zero(8, 128)],
        out_shape=[out, out, TOKEN],
        compiler_params=pltpu.CompilerParams(vmem_limit_bytes=16 * MIB),
        cost_estimate=STEP,
        name="split_sum",
    )(own[0], next_[0], got, got, after)


def third_kernel(at_ref, keep_ref, got_ref, after_ref, far_near_ref, next_own_ref, token_ref):
    for i in range(RING):
        rows = pl.ds(pl.multiple_of(at_ref[RING + i] * ROWS, ROWS), ROWS)
        total = (keep_ref[rows, :].astype(F32) + got_ref[rows, :].astype(F32)).astype(BF16)
        out_ref = far_near_ref if i < 2 else next_own_ref
        out_ref[i % 2 * ROWS : (i % 2 + 1) * ROWS, :] = total
    emit(token_ref)


def third_sum(at, keep, got, after, cost):
    width = keep.shape[1]
    return pl.pallas_call(
        third_kernel,
        grid_spec=pltpu.PrefetchScalarGridSpec(
            num_scalar_prefetch=1,
            grid=(1,),
            in_specs=[at_zero(CHUNK, width), at_zero(CHUNK, width), ANY],
            out_specs=[at_zero(2 * ROWS, width)] * 2 + [at_zero(8, 128)],
        ),
        out_shape=[jax.ShapeDtypeStruct((2 * ROWS, width), BF16)] * 2 + [TOKEN],
        compiler_params=pltpu.CompilerParams(vmem_limit_bytes=12 * MIB),
        cost_estimate=cost,
        name="third_sum",
    )(at, keep, got, after)


def fifth_kernel(keep_ref, got_ref, after_ref, out_ref, token_ref):
    out_ref[...] = keep_ref[...].astype(F32) + got_ref[...].astype(F32)
    emit(token_ref)


def fifth_sum(keep, got, after):
    width = keep.shape[1]
    block = at_zero(ROWS, width)
    return pl.pallas_call(
        fifth_kernel,
        grid=(1,),
        in_specs=[block, block, ANY],
        out_specs=[block, at_zero(8, 128)],
        out_shape=[jax.ShapeDtypeStruct((ROWS, width), F32), TOKEN],
        compiler_params=pltpu.CompilerParams(vmem_limit_bytes=4 * MIB),
        cost_estimate=STEP,
        name="fifth_sum",
    )(keep, got, after)


def combine_kernel(target_ref, weights_ref, back_ref, grads_ref, after_ref, mixed_ref, d_tokens_ref, d_route_ref, token_ref
):
    emit(token_ref)
    weights = weights_ref[...]
    slot = lax.broadcasted_iota(jnp.int32, (SLOTS, ROWS), 0)
    align = jnp.zeros((SLOTS, ROWS), F32)
    tiles = D // OUT_TILE
    for i in range(tiles):
        out = back_ref[:, 2 * i * OUT_TILE : (2 * i + 1) * OUT_TILE]
        align = align + dot(out, grads_ref[:, i * OUT_TILE : (i + 1) * OUT_TILE], (1, 1))
    chosen = jnp.zeros((SLOTS, ROWS), F32)
    scale = jnp.zeros((SLOTS, ROWS), F32)
    for k in range(TOP):
        here = target_ref[k : k + 1, :] == slot
        chosen = chosen + jnp.where(here, 1.0, 0.0)
        scale = scale + jnp.where(here, weights[k : k + 1, :], 0.0)
        d_route_ref[k : k + 1, :] = jnp.sum(jnp.where(here, align, 0.0), axis=0, keepdims=True)
    chosen = chosen.astype(BF16)
    high = scale.astype(BF16)
    low = (scale - high.astype(F32)).astype(BF16)
    for i in range(tiles):
        out = back_ref[:, 2 * i * OUT_TILE : (2 * i + 1) * OUT_TILE]
        d_in = back_ref[:, (2 * i + 1) * OUT_TILE : (2 * i + 2) * OUT_TILE]
        at = slice(i * OUT_TILE, (i + 1) * OUT_TILE)
        mixed_ref[:, at] = (dot(high, out, (0, 0)) + dot(low, out, (0, 0))).astype(BF16)
        d_tokens_ref[:, at] = dot(chosen, d_in, (0, 0)).astype(BF16)


def combine(target, weights, back, grads, after):
    whole = pl.BlockSpec(memory_space=pltpu.VMEM)
    return pl.pallas_call(
        combine_kernel,
        in_specs=[whole] * 4 + [ANY],
        out_shape=(
            jax.ShapeDtypeStruct((ROWS, D), BF16),
            jax.ShapeDtypeStruct((ROWS, D), BF16),
            jax.ShapeDtypeStruct((TOP, ROWS), F32),
            TOKEN,
        ),
        compiler_params=pltpu.CompilerParams(vmem_limit_bytes=20 * MIB),
        cost_estimate=SMALL,
        name="combine_rows",
    )(target, weights, back, grads, after)


def on_device(tokens, grad_out, expert_ids, route_weights, w_gate, w_up, w_down):
    x, z = lax.axis_index("dp") // RING, lax.axis_index("dp") % RING
    core = lax.axis_index("expert") % 2

    def chunk_order(at):
        beside, across = at ^ 1, RING - 1 - at
        first = jnp.where(core == 0, beside, across)
        second = jnp.where(core == 0, across, beside)
        return [(at + 2) % RING, first, second, at]

    at = jnp.stack(chunk_order(x) + chunk_order(z)).astype(jnp.int32)
    gate_w, up_w, down_w = w_gate[0], w_up[0], w_down[0]
    ids, weights = expert_ids.T, route_weights.T

    def exchange(buffer):
        buffer = buffer.reshape(EXPERTS, CAP, 2 * D)
        buffer = lax.all_to_all(buffer, "expert", split_axis=0, concat_axis=0, tiled=True)
        return buffer.reshape(SLOTS, 2 * D)

    def send_on(array, axis, stage):
        return lax.ppermute(array, ALL, pairs_of(axis, stage))

    send, target = place(at, ids, weights, tokens, grad_out)
    rows = exchange(send)
    hidden, d_gate, d_up = hidden_pass(rows, gate_w, up_w, down_w)

    factors = {"gate": (0, d_gate), "up": (0, d_up), "down": (1, hidden)}
    got, sums, grads = {}, {}, {}
    token = target
    back = None
    for step in ORDER:
        kind, name = step.split()
        if kind in ("first", "rest", "all"):
            side, factor = factors[name]
            start, count = {"first": (0, 2), "rest": (2, 2), "all": (0, 4)}[kind]
            *made, token = partial(at, rows, side, start, count, factor, 0, FF, token)
            if kind != "first":
                sums[name] = made[-1]
            if kind != "rest":
                got[name] = send_on(made[0], "x", 0)
        elif kind == "second":
            both = sums[name]
            send, sums[name], token = split_sum(CHUNK, (both, 1), (both, 0), got[name], token)
            got[name] = send_on(send, "x", 1)
        elif kind == "third":
            cost = LONG if name == "gate" else STEP
            send, sums[name], token = third_sum(at, sums[name], got[name], token, cost)
            got[name] = send_on(send, "z", 0)
        elif kind == "fourth":
            both = sums[name]
            send, sums[name], token = split_sum(ROWS, (both, 1), (both, 0), got[name], token)
            got[name] = send_on(send, "z", 1)
        elif kind == "fifth":
            total, token = fifth_sum(sums[name], got[name], token)
            grads[name] = total[None]
        elif name == "back":
            back, token = back_pass(hidden, d_gate, d_up, gate_w, up_w, down_w, token)
            back = exchange(back)
        else:
            mixed, d_tokens, d_route, token = combine(target, weights, back, grad_out, token)
    return (mixed, d_tokens, d_route.T) + tuple(grads[name] for name in ("gate", "up", "down"))


def solution(mesh):
    by_device = P(("dp", "expert"), None)
    by_expert = P("expert", None, None)
    by_row = P("expert", "dp", None)
    return jax.shard_map(
        on_device,
        mesh=mesh,
        in_specs=(by_device,) * 4 + (by_expert,) * 3,
        out_specs=(by_device,) * 3 + (by_row,) * 3,
        check_vma=False,
    )
```

```python
import jax
import jax.numpy as jnp
from jax import lax
from jax.experimental import pallas as pl
from jax.experimental.pallas import tpu as pltpu
from jax.sharding import PartitionSpec as P

CAP = 24
EXPERTS = 16
SLOTS = EXPERTS * CAP
ROWS = 128
TOP = 6
D = 2048
FF = 768
RING = 4
MIB = 1024 * 1024
LONG = pl.CostEstimate(flops=6 * 10**9, bytes_accessed=MIB, transcendentals=0)
STEP = pl.CostEstimate(flops=6 * 10**9, bytes_accessed=1, transcendentals=0)
SMALL = pl.CostEstimate(flops=1, bytes_accessed=1, transcendentals=0)
F32 = jnp.float32
BF16 = jnp.bfloat16
ALL = ("dp", "expert")
ORDER = (
    "first gate",
    "run back",
    "all up",
    "rest gate",
    "second gate",
    "all down",
    "third gate",
    "second up",
    "fourth gate",
    "third up",
    "second down",
    "fourth up",
    "fifth gate",
    "third down",
    "run combine",
    "fifth up",
    "fourth down",
    "fifth down",
)


def partners(core, at):
    beside, across = at ^ 1, RING - 1 - at
    first, second = (beside, across) if core == 0 else (across, beside)
    return first, second, (at + 2) % RING


def pairs_of(axis, stage):
    pairs = []
    for dp in range(RING * RING):
        x, z = divmod(dp, RING)
        for expert in range(EXPERTS):
            if axis == "x":
                to = partners(expert % 2, x)[stage] * RING + z
            else:
                to = x * RING + partners(expert % 2, z)[stage]
            pairs.append((dp * EXPERTS + expert, to * EXPERTS + expert))
    return pairs


def dot(a, b, contract):
    return lax.dot_general(a, b, ((contract[:1], contract[1:]), ((), ())), preferred_element_type=F32)


def place_kernel(at_ref, ids_ref, weights_ref, tokens_ref, grads_ref, send_ref, target_ref):
    ids = ids_ref[...]
    weights = weights_ref[...]
    expert = lax.broadcasted_iota(jnp.int32, (EXPERTS, ROWS), 0)
    picked = jnp.zeros((EXPERTS, ROWS), F32)
    for k in range(TOP):
        picked = picked + jnp.where(ids[k : k + 1, :] == expert, 1.0, 0.0)
    earlier = lax.broadcasted_iota(jnp.int32, (ROWS, ROWS), 0) < lax.broadcasted_iota(
        jnp.int32, (ROWS, ROWS), 1
    )
    position = jnp.dot(
        picked.astype(BF16),
        jnp.where(earlier, 1.0, 0.0).astype(BF16),
        preferred_element_type=F32,
    )
    slot = lax.broadcasted_iota(jnp.int32, (SLOTS, ROWS), 0)
    chosen = jnp.zeros((SLOTS, ROWS), F32)
    scale = jnp.zeros((SLOTS, ROWS), F32)
    for k in range(TOP):
        pick = ids[k : k + 1, :]
        own = jnp.sum(jnp.where(pick == expert, position, 0.0), axis=0, keepdims=True)
        place = own.astype(jnp.int32)
        target = jnp.where((pick < EXPERTS) & (place < CAP), pick * CAP + place, -1)
        target_ref[k : k + 1, :] = target
        here = target == slot
        chosen = chosen + jnp.where(here, 1.0, 0.0)
        scale = scale + jnp.where(here, weights[k : k + 1, :], 0.0)
    chosen = chosen.astype(BF16)
    slot_scale = jnp.sum(scale, axis=1, keepdims=True)
    send_ref[:, :D] = jnp.dot(chosen, tokens_ref[...], preferred_element_type=F32).astype(BF16)
    send_ref[:, D:] = (
        slot_scale * jnp.dot(chosen, grads_ref[...], preferred_element_type=F32)
    ).astype(BF16)


def place(at, ids, weights, tokens, grads):
    whole = pl.BlockSpec(memory_space=pltpu.VMEM)
    return pl.pallas_call(
        place_kernel,
        in_specs=[pl.BlockSpec(memory_space=pltpu.SMEM)] + [whole] * 4,
        out_shape=(
            jax.ShapeDtypeStruct((SLOTS, 2 * D), BF16),
            jax.ShapeDtypeStruct((TOP, ROWS), jnp.int32),
        ),
        compiler_params=pltpu.CompilerParams(vmem_limit_bytes=20 * MIB),
        cost_estimate=pl.CostEstimate(flops=4 * 10**10, bytes_accessed=5 * MIB, transcendentals=0),
        name="place_rows",
    )(at, ids, weights, tokens, grads)


def hidden_kernel(rows_ref, gate_ref, up_ref, down_ref, hidden_ref, d_gate_ref, d_up_ref):
    inputs = rows_ref[:, :D]
    gate_pre = jnp.dot(inputs, gate_ref[...], preferred_element_type=F32)
    up_pre = jnp.dot(inputs, up_ref[...], preferred_element_type=F32)
    d_hidden = jnp.dot(rows_ref[:, D:], down_ref[...], preferred_element_type=F32)
    sigmoid = jax.nn.sigmoid(gate_pre)
    silu = gate_pre * sigmoid
    hidden_ref[...] = (silu * up_pre).astype(BF16)
    d_up_ref[...] = (d_hidden * silu).astype(BF16)
    d_gate_ref[...] = (d_hidden * up_pre * sigmoid * (1.0 + gate_pre * (1.0 - sigmoid))).astype(BF16)


def hidden_pass(rows, gate_w, up_w, down_w):
    tile = 256
    weight = pl.BlockSpec((D, tile), lambda i: (0, i))
    out = pl.BlockSpec((SLOTS, tile), lambda i: (0, i))
    return pl.pallas_call(
        hidden_kernel,
        grid=(FF // tile,),
        in_specs=[pl.BlockSpec((SLOTS, 2 * D), lambda i: (0, 0)), weight, weight, weight],
        out_specs=[out] * 3,
        out_shape=[jax.ShapeDtypeStruct((SLOTS, FF), BF16)] * 3,
        compiler_params=pltpu.CompilerParams(vmem_limit_bytes=20 * MIB),
        cost_estimate=SMALL,
        name="hidden_pass",
    )(rows, gate_w, up_w, down_w)


OUT_TILE = 512
CHUNK = D // RING
ANY = pl.BlockSpec(memory_space=pl.ANY)
TOKEN = jax.ShapeDtypeStruct((8, 128), jnp.int32)


def at_zero(*shape):
    return pl.BlockSpec(shape, lambda *_: (0,) * len(shape))


def emit(token_ref):
    token_ref[...] = jnp.zeros(token_ref.shape, token_ref.dtype)


def back_kernel(
    hidden_ref, d_gate_ref, d_up_ref, gate_ref, up_ref, down_ref, after_ref, out_ref, token_ref
):
    out_ref[:, :OUT_TILE] = dot(hidden_ref[...], down_ref[...], (1, 1)).astype(BF16)
    out_ref[:, OUT_TILE:] = (
        dot(d_gate_ref[...], gate_ref[...], (1, 1)) + dot(d_up_ref[...], up_ref[...], (1, 1))
    ).astype(BF16)
    emit(token_ref)


def back_pass(hidden, d_gate, d_up, gate_w, up_w, down_w, after):
    act = at_zero(SLOTS, FF)
    weight = pl.BlockSpec((OUT_TILE, FF), lambda i: (i, 0))
    return pl.pallas_call(
        back_kernel,
        grid=(D // OUT_TILE,),
        in_specs=[act, act, act, weight, weight, weight, ANY],
        out_specs=[pl.BlockSpec((SLOTS, 2 * OUT_TILE), lambda i: (0, i)), at_zero(8, 128)],
        out_shape=[jax.ShapeDtypeStruct((SLOTS, 2 * D), BF16), TOKEN],
        compiler_params=pltpu.CompilerParams(vmem_limit_bytes=20 * MIB),
        cost_estimate=SMALL,
        name="back_pass",
    )(hidden, d_gate, d_up, gate_w, up_w, down_w, after)


def partial_kernel(at_ref, lhs_ref, rhs_ref, after_ref, *refs):
    value = dot(lhs_ref[...], rhs_ref[...], (0, 0)).astype(BF16)
    *out_refs, token_ref = refs
    for i, out_ref in enumerate(out_refs):
        if len(out_refs) == 1:
            out_ref[...] = value
        else:

            @pl.when(pl.program_id(0) // 2 == i)
            def _():
                out_ref[...] = value

    emit(token_ref)


def partial(at, rows, side, first, count, grads, column, width, after):
    def out_spec(i):
        return pl.BlockSpec(
            (CHUNK, width), lambda s, at: (jnp.clip(s - 2 * i, 0, 1) if count > 2 else s, 0)
        )

    outs = count // 2
    return pl.pallas_call(
        partial_kernel,
        grid_spec=pltpu.PrefetchScalarGridSpec(
            num_scalar_prefetch=1,
            grid=(count,),
            in_specs=[
                pl.BlockSpec((SLOTS, CHUNK), lambda s, at: (0, side * RING + at[first + s])),
                pl.BlockSpec((SLOTS, width), lambda s, at: (0, column)),
                ANY,
            ],
            out_specs=[out_spec(i) for i in range(outs)] + [at_zero(8, 128)],
        ),
        out_shape=[jax.ShapeDtypeStruct((2 * CHUNK, width), BF16)] * outs + [TOKEN],
        compiler_params=pltpu.CompilerParams(vmem_limit_bytes=12 * MIB),
        cost_estimate=SMALL,
        name="partial",
    )(at, rows, grads, after)


def split_kernel(own_ref, next_ref, got_next_ref, got_own_ref, after_ref, send_ref, keep_ref, token_ref):
    send_ref[...] = (next_ref[...].astype(F32) + got_next_ref[...].astype(F32)).astype(BF16)
    keep_ref[...] = (own_ref[...].astype(F32) + got_own_ref[...].astype(F32)).astype(BF16)
    emit(token_ref)


def split_sum(rows, own, next_, got, after):
    width = got.shape[1]

    def block(i):
        return pl.BlockSpec((rows, width), lambda s: (i, 0))

    out = jax.ShapeDtypeStruct((rows, width), BF16)
    return pl.pallas_call(
        split_kernel,
        grid=(1,),
        in_specs=[block(own[1]), block(next_[1]), block(0), block(1), ANY],
        out_specs=[block(0), block(0), at_zero(8, 128)],
        out_shape=[out, out, TOKEN],
        compiler_params=pltpu.CompilerParams(vmem_limit_bytes=16 * MIB),
        cost_estimate=STEP,
        name="split_sum",
    )(own[0], next_[0], got, got, after)


def third_kernel(at_ref, keep_ref, got_ref, after_ref, far_near_ref, next_own_ref, token_ref):
    for i in range(RING):
        rows = pl.ds(pl.multiple_of(at_ref[RING + i] * ROWS, ROWS), ROWS)
        total = (keep_ref[rows, :].astype(F32) + got_ref[rows, :].astype(F32)).astype(BF16)
        out_ref = far_near_ref if i < 2 else next_own_ref
        out_ref[i % 2 * ROWS : (i % 2 + 1) * ROWS, :] = total
    emit(token_ref)


def third_sum(at, keep, got, after, cost):
    width = keep.shape[1]
    return pl.pallas_call(
        third_kernel,
        grid_spec=pltpu.PrefetchScalarGridSpec(
            num_scalar_prefetch=1,
            grid=(1,),
            in_specs=[at_zero(CHUNK, width), at_zero(CHUNK, width), ANY],
            out_specs=[at_zero(2 * ROWS, width)] * 2 + [at_zero(8, 128)],
        ),
        out_shape=[jax.ShapeDtypeStruct((2 * ROWS, width), BF16)] * 2 + [TOKEN],
        compiler_params=pltpu.CompilerParams(vmem_limit_bytes=12 * MIB),
        cost_estimate=cost,
        name="third_sum",
    )(at, keep, got, after)


def fifth_kernel(keep_ref, got_ref, after_ref, out_ref, token_ref):
    out_ref[...] = keep_ref[...].astype(F32) + got_ref[...].astype(F32)
    emit(token_ref)


def fifth_sum(keep, got, after):
    width = keep.shape[1]
    block = at_zero(ROWS, width)
    return pl.pallas_call(
        fifth_kernel,
        grid=(1,),
        in_specs=[block, block, ANY],
        out_specs=[block, at_zero(8, 128)],
        out_shape=[jax.ShapeDtypeStruct((ROWS, width), F32), TOKEN],
        compiler_params=pltpu.CompilerParams(vmem_limit_bytes=4 * MIB),
        cost_estimate=STEP,
        name="fifth_sum",
    )(keep, got, after)


def combine_kernel(target_ref, weights_ref, back_ref, grads_ref, after_ref, mixed_ref, d_tokens_ref, d_route_ref, token_ref
):
    emit(token_ref)
    weights = weights_ref[...]
    slot = lax.broadcasted_iota(jnp.int32, (SLOTS, ROWS), 0)
    align = jnp.zeros((SLOTS, ROWS), F32)
    tiles = D // OUT_TILE
    for i in range(tiles):
        out = back_ref[:, 2 * i * OUT_TILE : (2 * i + 1) * OUT_TILE]
        align = align + dot(out, grads_ref[:, i * OUT_TILE : (i + 1) * OUT_TILE], (1, 1))
    chosen = jnp.zeros((SLOTS, ROWS), F32)
    scale = jnp.zeros((SLOTS, ROWS), F32)
    for k in range(TOP):
        here = target_ref[k : k + 1, :] == slot
        chosen = chosen + jnp.where(here, 1.0, 0.0)
        scale = scale + jnp.where(here, weights[k : k + 1, :], 0.0)
        d_route_ref[k : k + 1, :] = jnp.sum(jnp.where(here, align, 0.0), axis=0, keepdims=True)
    chosen = chosen.astype(BF16)
    high = scale.astype(BF16)
    low = (scale - high.astype(F32)).astype(BF16)
    for i in range(tiles):
        out = back_ref[:, 2 * i * OUT_TILE : (2 * i + 1) * OUT_TILE]
        d_in = back_ref[:, (2 * i + 1) * OUT_TILE : (2 * i + 2) * OUT_TILE]
        at = slice(i * OUT_TILE, (i + 1) * OUT_TILE)
        mixed_ref[:, at] = (dot(high, out, (0, 0)) + dot(low, out, (0, 0))).astype(BF16)
        d_tokens_ref[:, at] = dot(chosen, d_in, (0, 0)).astype(BF16)


def combine(target, weights, back, grads, after):
    whole = pl.BlockSpec(memory_space=pltpu.VMEM)
    return pl.pallas_call(
        combine_kernel,
        in_specs=[whole] * 4 + [ANY],
        out_shape=(
            jax.ShapeDtypeStruct((ROWS, D), BF16),
            jax.ShapeDtypeStruct((ROWS, D), BF16),
            jax.ShapeDtypeStruct((TOP, ROWS), F32),
            TOKEN,
        ),
        compiler_params=pltpu.CompilerParams(vmem_limit_bytes=20 * MIB),
        cost_estimate=SMALL,
        name="combine_rows",
    )(target, weights, back, grads, after)


def on_device(tokens, grad_out, expert_ids, route_weights, w_gate, w_up, w_down):
    x, z = lax.axis_index("dp") // RING, lax.axis_index("dp") % RING
    core = lax.axis_index("expert") % 2

    def chunk_order(at):
        beside, across = at ^ 1, RING - 1 - at
        first = jnp.where(core == 0, beside, across)
        second = jnp.where(core == 0, across, beside)
        return [(at + 2) % RING, first, second, at]

    at = jnp.stack(chunk_order(x) + chunk_order(z)).astype(jnp.int32)
    gate_w, up_w, down_w = w_gate[0], w_up[0], w_down[0]
    ids, weights = expert_ids.T, route_weights.T

    def exchange(buffer):
        buffer = buffer.reshape(EXPERTS, CAP, 2 * D)
        buffer = lax.all_to_all(buffer, "expert", split_axis=0, concat_axis=0, tiled=True)
        return buffer.reshape(SLOTS, 2 * D)

    def send_on(array, axis, stage):
        return lax.ppermute(array, ALL, pairs_of(axis, stage))

    send, target = place(at, ids, weights, tokens, grad_out)
    rows = exchange(send)
    hidden, d_gate, d_up = hidden_pass(rows, gate_w, up_w, down_w)

    factors = {"gate": (0, d_gate), "up": (0, d_up), "down": (1, hidden)}
    got, sums, grads = {}, {}, {}
    token = target
    back = None
    for step in ORDER:
        kind, name = step.split()
        if kind in ("first", "rest", "all"):
            side, factor = factors[name]
            start, count = {"first": (0, 2), "rest": (2, 2), "all": (0, 4)}[kind]
            *made, token = partial(at, rows, side, start, count, factor, 0, FF, token)
            if kind != "first":
                sums[name] = made[-1]
            if kind != "rest":
                got[name] = send_on(made[0], "x", 0)
        elif kind == "second":
            both = sums[name]
            send, sums[name], token = split_sum(CHUNK, (both, 1), (both, 0), got[name], token)
            got[name] = send_on(send, "x", 1)
        elif kind == "third":
            cost = LONG if name == "gate" else STEP
            send, sums[name], token = third_sum(at, sums[name], got[name], token, cost)
            got[name] = send_on(send, "z", 0)
        elif kind == "fourth":
            both = sums[name]
            send, sums[name], token = split_sum(ROWS, (both, 1), (both, 0), got[name], token)
            got[name] = send_on(send, "z", 1)
        elif kind == "fifth":
            total, token = fifth_sum(sums[name], got[name], token)
            grads[name] = total[None]
        elif name == "back":
            back, token = back_pass(hidden, d_gate, d_up, gate_w, up_w, down_w, token)
            back = exchange(back)
        else:
            mixed, d_tokens, d_route, token = combine(target, weights, back, grad_out, token)
    return (mixed, d_tokens, d_route.T) + tuple(grads[name] for name in ("gate", "up", "down"))


def solution(mesh):
    by_device = P(("dp", "expert"), None)
    by_expert = P("expert", None, None)
    by_row = P("expert", "dp", None)
    return jax.shard_map(
        on_device,
        mesh=mesh,
        in_specs=(by_device,) * 4 + (by_expert,) * 3,
        out_specs=(by_device,) * 3 + (by_row,) * 3,
        check_vma=False,
    )
```
